32 devices in a mesh: replica: 2 (over x), fsdp: 16 (over z, y, core).
Axes of the slice: x: 2, y: 2, z: 4, core: 2. Of those that a mesh axis runs over, the one named last changes fastest.
Arguments:
- tokens: bfloat16 [4096, 8192], P(('replica', 'fsdp')), may hold values from -400 to 400
- cotangent: bfloat16 [4096, 512], P(('replica', 'fsdp')), may hold values from -6 to 6
- gain: float32 [2, 8192], P('replica'), may hold values from 0.1 to 1.9
- local_weight: float32 [2, 8192, 512], P('replica', 'fsdp'), may hold values from -6 to 6
- stale_weight: float32 [2, 8192, 512], P('replica', 'fsdp'), may hold values from -6 to 6
- global_weight: float32 [8192, 512], P('fsdp'), may hold values from -6 to 6
- momentum: float32 [8192, 512], P('fsdp'), may hold values from -3 to 3
Outputs:
- local_new: float32 [2, 8192, 512], P('replica', 'fsdp')
- gain_new: float32 [2, 8192], P('replica')
- global_new: float32 [8192, 512], P('fsdp')
- momentum_new: float32 [8192, 512], P('fsdp')
The draws below stay inside these ranges and needn't reach their ends.
All inputs are finite; a program needn't handle non-finite values.
Results may differ from the reference program's by a relative error of at most 0.00053.
Values may be sent and summed in bfloat16 or wider, within the bound.
A program may use at most 64 MiB of HBM per device.

```python
import math
import jax
import jax.numpy as jnp
from jax import lax

D = 8192
HEAD = 128
KV_HEADS = 4
KV = 512
TOK_REP = 2048
TOKENS = 4096
N_REPLICA = 2


def draw_tokens(key, part):
    key = jax.random.fold_in(key, 11)
    first, second, third = jax.random.split(key, 3)
    row_scale = jnp.exp(jax.random.uniform(second, (TOKENS, 1), jnp.float32, 0.0, math.log(10.0)))
    col_scale = jnp.exp(jax.random.uniform(third, (1, D), jnp.float32, math.log(0.5), math.log(2.0)))
    base = jnp.clip(jax.random.normal(first, (TOKENS, D), jnp.float32), -6.0, 6.0)
    return (base * row_scale * col_scale).astype(jnp.bfloat16)


def levels(key, dims, cuts, smallest, top_value):
    def one(position, blocks):
        draws = jax.random.uniform(jax.random.fold_in(jax.random.fold_in(key, 6), position), (blocks,), jnp.float32, smallest / len(cuts), top_value / len(cuts))
        return jnp.repeat(jnp.exp(draws), dims[position] // blocks).reshape((-1,) + (1,) * (len(dims) - position - 1))

    factor_of = one(*cuts[0])
    for cut in cuts[1:]:
        factor_of = factor_of * one(*cut)
    return factor_of


def gaussian(stream_key, extent, deviation, bound, cuts=(), dtype=jnp.bfloat16):
    level = levels(stream_key, extent, cuts, -0.22, 0.18) if cuts else 1.0
    array = jax.random.normal(stream_key, extent, jnp.float32) * deviation * level
    return jnp.minimum(jnp.maximum(array, -bound), bound).astype(dtype)


def setup_inputs(seed: int = 0) -> dict:
    arg_keys = jax.random.split(jax.random.key(seed), 8)
    return {
        "tokens": draw_tokens(jax.random.fold_in(arg_keys[7], 71), 0),
        "cotangent": gaussian(arg_keys[1], (TOKENS, KV), 1.0, 6.0, ((0, 32),)),
        "gain": jnp.clip(1.0 + 0.18 * jax.random.normal(arg_keys[2], (N_REPLICA, D), jnp.float32), 0.1, 1.9),
        "local_weight": gaussian(arg_keys[3], (N_REPLICA, D, KV), 1.0, 6.0, ((0, 2), (1, 16)), jnp.float32),
        "stale_weight": gaussian(arg_keys[4], (N_REPLICA, D, KV), 1.0, 6.0, ((0, 2), (1, 16)), jnp.float32),
        "global_weight": gaussian(arg_keys[5], (D, KV), 1.0, 6.0, ((0, 16),), jnp.float32),
        "momentum": gaussian(arg_keys[6], (D, KV), 0.5, 3.0, ((0, 16),), jnp.float32),
    }


EPS = 1e-05
LR_INNER = 0.3
LR_GAIN = 0.01
LR_OUTER = 0.7
MOMENT = 0.9
MIXING = 0.5

def head_backward(keys, cot32):
    rows = keys.shape[0]
    keys_h = keys.reshape(rows, KV_HEADS, HEAD)
    cot_h = cot32.reshape(rows, KV_HEADS, HEAD)
    key_scale = lax.rsqrt(lax.optimization_barrier(jnp.mean(keys_h * keys_h, axis=2, keepdims=True)) + EPS)
    unit_keys = keys_h * key_scale
    along = lax.optimization_barrier(jnp.mean(cot_h * unit_keys, axis=2, keepdims=True))
    return (key_scale * (cot_h - unit_keys * along)).reshape(rows, KV_HEADS * HEAD).astype(jnp.bfloat16)

def one_replica(items):
    tok_block, cot_block, gain_row, weight = items
    factor = D ** (-0.5)
    tok32 = tok_block.astype(jnp.float32)
    inv_rms = lax.rsqrt(lax.optimization_barrier(jnp.mean(tok32 * tok32, axis=1, keepdims=True)) + EPS)
    scaled = tok32 * inv_rms
    normed = (scaled * gain_row[None, :]).astype(jnp.bfloat16)
    weight_bf = weight.astype(jnp.bfloat16)
    keys = jnp.dot(normed, weight_bf, preferred_element_type=jnp.float32) * factor
    dproj = head_backward(keys, cot_block.astype(jnp.float32))
    dnormed = jnp.dot(dproj, weight_bf.T, preferred_element_type=jnp.float32) * factor
    gain_grad = lax.optimization_barrier(jnp.sum(scaled * dnormed, axis=0))
    weight_grad = jnp.dot(normed.T, dproj, preferred_element_type=jnp.float32) * factor
    return (weight - LR_INNER * weight_grad, gain_row - LR_GAIN * gain_grad)

def reference(tokens, cotangent, gain, local_weight, stale_weight, global_weight, momentum):
    tok_all = tokens.reshape(N_REPLICA, TOK_REP, D)
    cot_all = cotangent.reshape(N_REPLICA, TOK_REP, KV)
    inner, gain_new = lax.map(one_replica, (tok_all, cot_all, gain, local_weight))
    outer_mean = lax.optimization_barrier(jnp.sum(global_weight[None] - stale_weight, axis=0)) / N_REPLICA
    momentum_new = MOMENT * momentum + outer_mean
    global_new = global_weight - LR_OUTER * (outer_mean + MOMENT * momentum_new)
    local_new = MIXING * inner + (1.0 - MIXING) * global_new[None]
    return (local_new, gain_new, global_new, momentum_new)
```

```python
import functools

import jax
import jax.numpy as jnp
from jax import lax
from jax.experimental import pallas as pl
from jax.experimental.pallas import tpu as pltpu
from jax.sharding import PartitionSpec as P

HEAD = 128
KV_HEADS = 4


EPS = 1e-05
LR_INNER = 0.3
LR_GAIN = 0.01
LR_OUTER = 0.7
MOMENT = 0.9
MIXING = 0.5

MESH = pl.DeviceIdType.MESH
PLANE = 4


def head_backward(keys, cot32):
    parts = []
    for h in range(KV_HEADS):
        cols = slice(h * HEAD, (h + 1) * HEAD)
        keys_h = keys[:, cols]
        cot_h = cot32[:, cols]
        key_scale = lax.rsqrt(jnp.mean(keys_h * keys_h, axis=1, keepdims=True) + EPS)
        unit_keys = keys_h * key_scale
        along = jnp.mean(cot_h * unit_keys, axis=1, keepdims=True)
        parts.append((key_scale * (cot_h - unit_keys * along)).astype(jnp.bfloat16))
    return jnp.concatenate(parts, axis=1)


def kernel(
    n, n_rep, factor,
    tok_ref, cot_ref, gain_ref, weight_ref, stale_ref, global_ref, mom_ref,
    local_out, gain_out, global_out, mom_out,
    normed_buf, x_all, w_bf, part_f32, part_bf, plane_recv, keys_send, keys_recv,
    keys_acc, dproj_all, grad_acc, delta_buf, delta_recv, gain_buf,
    x_send_sem, x_recv_sem, plane_send_sem, plane_recv_sem, keys_send_sem,
    keys_recv_sem, dproj_send_sem, dproj_recv_sem, delta_send_sem, delta_recv_sem,
    gain_send_sem, gain_recv_sem,
):
    rep = lax.axis_index("replica")
    me = lax.axis_index("fsdp")
    planes = n // PLANE
    z, q = me // PLANE, me % PLANE
    rows = tok_ref.shape[0]
    feats = weight_ref.shape[0]

    def at(plane, place):
        return plane * PLANE + place

    def turned(d):
        return lax.rem(z + d, planes)

    def send(src, dst, send_sem, recv_sem, target, replica=None):
        pltpu.make_async_remote_copy(
            src_ref=src, dst_ref=dst, send_sem=send_sem, recv_sem=recv_sem,
            device_id=(rep if replica is None else replica, target), device_id_type=MESH,
        ).start()

    def wait_bytes(ref, sem):
        pltpu.make_async_copy(ref, ref, sem).wait()

    barrier = pltpu.get_barrier_semaphore()
    for i in range(1, n):
        pl.semaphore_signal(
            barrier, inc=1, device_id=(rep, lax.rem(me + i, n)), device_id_type=MESH
        )
    for i in range(1, n_rep):
        pl.semaphore_signal(
            barrier, inc=1, device_id=(lax.rem(rep + i, n_rep), me), device_id_type=MESH
        )

    total = jnp.zeros((rows, 1), jnp.float32)
    for j in range(n):
        piece = tok_ref[:, j * feats:(j + 1) * feats].astype(jnp.float32)
        total += jnp.sum(piece * piece, axis=1, keepdims=True)
    inv_rms = lax.rsqrt(total / tok_ref.shape[1] + EPS)
    for j in range(n):
        cols = slice(j * feats, (j + 1) * feats)
        scaled = tok_ref[:, cols].astype(jnp.float32) * inv_rms
        normed_buf[j] = (scaled * gain_ref[:, cols]).astype(jnp.bfloat16)
    pl.semaphore_wait(barrier, n - 1 + n_rep - 1)

    def block_rows(index):
        return pl.ds(pl.multiple_of(index * rows, rows), rows)

    def plane_rows(plane):
        return pl.ds(pl.multiple_of(plane * (PLANE * rows), PLANE * rows), PLANE * rows)

    for d in range(planes):
        for e in range(PLANE):
            if d == 0 and e == 0:
                continue
            target = at(turned(d), lax.rem(q + e, PLANE))
            send(normed_buf.at[target], x_all.at[block_rows(me), :], x_send_sem,
                 x_recv_sem.at[z], target)
    delta_buf[...] = global_ref[...] - stale_ref[...]
    for i in range(1, n_rep):
        send(delta_buf, delta_recv.at[i - 1], delta_send_sem, delta_recv_sem, me,
             lax.rem(rep + i, n_rep))
    x_all[block_rows(me), :] = normed_buf[me]
    w_bf[...] = weight_ref[...].astype(jnp.bfloat16)

    def partial_keys(d):
        plane = turned(planes - d)
        count = PLANE - 1 if d == 0 else PLANE
        wait_bytes(x_all.at[pl.ds(0, count * rows), :], x_recv_sem.at[plane])
        part = jnp.dot(x_all[plane_rows(plane), :], w_bf[...],
                       preferred_element_type=jnp.float32)
        part_f32[d] = part
        part_bf[d] = part.astype(jnp.bfloat16)
        for e in range(1, PLANE):
            place = lax.rem(q + e, PLANE)
            send(part_bf.at[d, block_rows(place), :], plane_recv.at[d, e - 1],
                 plane_send_sem, plane_recv_sem.at[d], at(z, place))

    def plane_sum(d):
        wait_bytes(plane_recv.at[d], plane_recv_sem.at[d])
        summed = part_f32[d, block_rows(q), :]
        for e in range(PLANE - 1):
            summed += plane_recv[d, e].astype(jnp.float32)
        if d == 0:
            keys_acc[...] = summed
        else:
            keys_send[d - 1] = summed.astype(jnp.bfloat16)
            send(keys_send.at[d - 1], keys_recv.at[d - 1], keys_send_sem,
                 keys_recv_sem, at(turned(planes - d), q))

    partial_keys(0)
    for d in range(1, planes):
        partial_keys(d)
        plane_sum(d - 1)
    plane_sum(planes - 1)

    wait_bytes(delta_recv, delta_recv_sem)
    outer = delta_buf[...]
    for i in range(n_rep - 1):
        outer += delta_recv[i]
    outer_mean = outer / n_rep
    momentum_new = MOMENT * mom_ref[...] + outer_mean
    global_new = global_ref[...] - LR_OUTER * (outer_mean + MOMENT * momentum_new)
    mom_out[...] = momentum_new
    global_out[...] = global_new
    local_out[...] = MIXING * weight_ref[...] + (1.0 - MIXING) * global_new

    wait_bytes(keys_recv, keys_recv_sem)
    keys = keys_acc[...]
    for d in range(planes - 1):
        keys += keys_recv[d].astype(jnp.float32)
    dproj_all[block_rows(me), :] = head_backward(
        keys * factor, cot_ref[...].astype(jnp.float32)
    )

    pair = lax.rem(q + 2, PLANE)
    core = q + 1 - 2 * lax.rem(q, 2)
    last = lax.rem(core + 2, PLANE)

    def pass_on(index, target):
        block = dproj_all.at[block_rows(index), :]
        send(block, block, dproj_send_sem, dproj_recv_sem.at[index], target)

    def arrived(index):
        wait_bytes(dproj_all.at[block_rows(index), :], dproj_recv_sem.at[index])

    for d in range(1, planes):
        pass_on(me, at(turned(d), q))
    pass_on(me, at(z, pair))
    pass_on(me, at(z, core))

    def from_plane(d):
        index = at(turned(planes - d), q)
        arrived(index)
        pass_on(index, at(z, pair))
        pass_on(index, at(z, core))

    def from_pair(d):
        index = at(turned(planes - d), pair)
        arrived(index)
        pass_on(index, at(z, core))

    def add_plane(d):
        plane = turned(planes - d)
        arrived(at(plane, core))
        arrived(at(plane, last))
        product = lax.dot_general(
            x_all[plane_rows(plane), :], dproj_all[plane_rows(plane), :],
            (((0,), (0,)), ((), ())), preferred_element_type=jnp.float32,
        )
        if d == 0:
            grad_acc[...] = product
        else:
            grad_acc[...] += product

    for d in range(1, planes + 2):
        if d < planes:
            from_plane(d)
        if d - 1 < planes:
            from_pair(d - 1)
        if d >= 2:
            add_plane(d - 2)

    grad = grad_acc[...] * factor
    ones = jnp.ones((8, grad.shape[1]), jnp.float32)
    row = lax.dot_general(
        ones, w_bf[...].astype(jnp.float32) * grad, (((1,), (1,)), ((), ())),
        precision=lax.Precision.HIGHEST, preferred_element_type=jnp.float32,
    )[0:1, :]
    gain_own = gain_ref[:, pl.ds(pl.multiple_of(me * feats, feats), feats)]
    gain_buf[me] = gain_own - LR_GAIN * (row / gain_own)
    for i in range(1, n):
        send(gain_buf.at[me], gain_buf.at[me], gain_send_sem, gain_recv_sem,
             lax.rem(me + i, n))
    local_out[...] -= MIXING * LR_INNER * grad

    wait_bytes(normed_buf.at[pl.ds(0, n - 1)], x_send_sem)
    wait_bytes(plane_recv, plane_send_sem)
    wait_bytes(keys_send, keys_send_sem)
    wait_bytes(dproj_all.at[pl.ds(0, (n - 1) * rows), :], dproj_send_sem)
    wait_bytes(delta_recv, delta_send_sem)
    wait_bytes(gain_buf.at[pl.ds(0, n - 1)], gain_recv_sem)
    for j in range(n):
        gain_out[:, j * feats:(j + 1) * feats] = gain_buf[j]
    wait_bytes(gain_buf.at[pl.ds(0, n - 1)], gain_send_sem)


def body(tokens, cotangent, gain, local_weight, stale_weight, global_weight, momentum):
    n = lax.axis_size("fsdp")
    n_rep = lax.axis_size("replica")
    rows, width = tokens.shape
    feats, units = global_weight.shape
    planes = n // PLANE
    factor = width ** (-0.5)
    f32, bf16 = jnp.float32, jnp.bfloat16
    vmem = pl.BlockSpec(memory_space=pltpu.VMEM)
    dma = pltpu.SemaphoreType.DMA
    local_new, gain_new, global_new, momentum_new = pl.pallas_call(
        functools.partial(kernel, n, n_rep, factor),
        out_shape=(
            jax.ShapeDtypeStruct((feats, units), f32),
            jax.ShapeDtypeStruct((1, width), f32),
            jax.ShapeDtypeStruct((feats, units), f32),
            jax.ShapeDtypeStruct((feats, units), f32),
        ),
        in_specs=[vmem] * 7,
        out_specs=(vmem,) * 4,
        scratch_shapes=[
            pltpu.VMEM((n, rows, feats), bf16),
            pltpu.VMEM((n * rows, feats), bf16),
            pltpu.VMEM((feats, units), bf16),
            pltpu.VMEM((planes, PLANE * rows, units), f32),
            pltpu.VMEM((planes, PLANE * rows, units), bf16),
            pltpu.VMEM((planes, PLANE - 1, rows, units), bf16),
            pltpu.VMEM((planes - 1, rows, units), bf16),
            pltpu.VMEM((planes - 1, rows, units), bf16),
            pltpu.VMEM((rows, units), f32),
            pltpu.VMEM((n * rows, units), bf16),
            pltpu.VMEM((feats, units), f32),
            pltpu.VMEM((feats, units), f32),
            pltpu.VMEM((n_rep - 1, feats, units), f32),
            pltpu.VMEM((n, 1, feats), f32),
            dma, dma((planes,)),
            dma, dma((planes,)),
            dma, dma,
            dma, dma((n,)),
            dma, dma,
            dma, dma,
        ],
        compiler_params=pltpu.CompilerParams(
            collective_id=0, has_side_effects=True, vmem_limit_bytes=58 * 1024 * 1024
        ),
        name="diloco_step",
    )(
        tokens, cotangent, gain, local_weight[0], stale_weight[0], global_weight, momentum
    )
    return (local_new[None], gain_new, global_new, momentum_new)


def solution(mesh):
    return jax.shard_map(
        body,
        mesh=mesh,
        in_specs=(
            P(("replica", "fsdp"), None),
            P(("replica", "fsdp"), None),
            P("replica", None),
            P("replica", "fsdp", None),
            P("replica", "fsdp", None),
            P("fsdp", None),
            P("fsdp", None),
        ),
        out_specs=(
            P("replica", "fsdp", None),
            P("replica", None),
            P("fsdp", None),
            P("fsdp", None),
        ),
        check_vma=False,
    )
```

```python
import functools

import jax
import jax.numpy as jnp
from jax import lax
from jax.experimental import pallas as pl
from jax.experimental.pallas import tpu as pltpu
from jax.sharding import PartitionSpec as P

HEAD = 128
KV_HEADS = 4


EPS = 1e-05
LR_INNER = 0.3
LR_GAIN = 0.01
LR_OUTER = 0.7
MOMENT = 0.9
MIXING = 0.5

MESH = pl.DeviceIdType.MESH
PLANE = 4


def head_backward(keys, cot32):
    parts = []
    for h in range(KV_HEADS):
        cols = slice(h * HEAD, (h + 1) * HEAD)
        keys_h = keys[:, cols]
        cot_h = cot32[:, cols]
        key_scale = lax.rsqrt(jnp.mean(keys_h * keys_h, axis=1, keepdims=True) + EPS)
        unit_keys = keys_h * key_scale
        along = jnp.mean(cot_h * unit_keys, axis=1, keepdims=True)
        parts.append((key_scale * (cot_h - unit_keys * along)).astype(jnp.bfloat16))
    return jnp.concatenate(parts, axis=1)


def kernel(
    n, n_rep, factor,
    tok_ref, cot_ref, gain_ref, weight_hbm, stale_hbm, global_hbm,
    grad_out, gain_out, outer_out,
    weight_ref, stale_ref, global_ref,
    normed_buf, x_all, w_bf, part_f32, part_bf, core_recv, pair_send, pair_recv, keys_send, keys_recv,
    keys_acc, dproj_all, grad_acc, delta_buf, delta_recv, gain_buf,
    x_send_sem, x_recv_sem, core_send_sem, core_recv_sem, pair_send_sem, pair_recv_sem, keys_send_sem,
    keys_recv_sem, dproj_send_sem, dproj_recv_sem, delta_send_sem, delta_recv_sem,
    gain_send_sem, gain_recv_sem, load_sem,
):
    rep = lax.axis_index("replica")
    me = lax.axis_index("fsdp")
    planes = n // PLANE
    z, q = me // PLANE, me % PLANE
    pair = lax.rem(q + 2, PLANE)
    core = q + 1 - 2 * lax.rem(q, 2)
    last = lax.rem(core + 2, PLANE)
    rows = tok_ref.shape[0]
    feats = weight_hbm.shape[0]

    def at(plane, place):
        return plane * PLANE + place

    def across(m):
        plane, bit = z, 1
        while bit < planes:
            if m & bit:
                plane = plane + bit - 2 * bit * lax.rem(z // bit, 2)
            bit *= 2
        return plane

    half = planes // 2
    order = [*range(half, planes), *range(1, half)]

    def send(src, dst, send_sem, recv_sem, target, replica=None):
        pltpu.make_async_remote_copy(
            src_ref=src, dst_ref=dst, send_sem=send_sem, recv_sem=recv_sem,
            device_id=(rep if replica is None else replica, target), device_id_type=MESH,
        ).start()

    def wait_bytes(ref, sem):
        pltpu.make_async_copy(ref, ref, sem).wait()

    barrier = pltpu.get_barrier_semaphore()
    for i in range(1, n):
        pl.semaphore_signal(
            barrier, inc=1, device_id=(rep, lax.rem(me + i, n)), device_id_type=MESH
        )
    for i in range(1, n_rep):
        pl.semaphore_signal(
            barrier, inc=1, device_id=(lax.rem(rep + i, n_rep), me), device_id_type=MESH
        )

    loads = [
        pltpu.make_async_copy(src, dst, load_sem.at[i])
        for i, (src, dst) in enumerate(
            ((weight_hbm, weight_ref), (stale_hbm, stale_ref), (global_hbm, global_ref))
        )
    ]
    for load in loads:
        load.start()

    total = jnp.zeros((rows, 1), jnp.float32)
    for j in range(n):
        piece = tok_ref[:, j * feats:(j + 1) * feats].astype(jnp.float32)
        total += jnp.sum(piece * piece, axis=1, keepdims=True)
    inv_rms = lax.rsqrt(total / tok_ref.shape[1] + EPS)

    def normalize(index):
        cols = pl.ds(pl.multiple_of(index * feats, feats), feats)
        scaled = tok_ref[:, cols].astype(jnp.float32) * inv_rms
        return (scaled * gain_ref[:, cols]).astype(jnp.bfloat16)

    pl.semaphore_wait(barrier, n - 1 + n_rep - 1)

    def block_rows(index):
        return pl.ds(pl.multiple_of(index * rows, rows), rows)

    def plane_rows(plane):
        return pl.ds(pl.multiple_of(plane * (PLANE * rows), PLANE * rows), PLANE * rows)

    for d in [*order, 0]:
        for e in range(PLANE):
            if d == 0 and e == 0:
                continue
            target = at(across(d), lax.rem(q + e, PLANE))
            normed_buf[target] = normalize(target)
            send(normed_buf.at[target], x_all.at[block_rows(me), :], x_send_sem,
                 x_recv_sem.at[z], target)
    for load in loads:
        load.wait()
    delta_buf[...] = global_ref[...] - stale_ref[...]
    for i in range(1, n_rep):
        send(delta_buf, delta_recv.at[i - 1], delta_send_sem, delta_recv_sem, me,
             lax.rem(rep + i, n_rep))
    x_all[block_rows(me), :] = normalize(me)
    w_bf[...] = weight_ref[...].astype(jnp.bfloat16)

    def partial_keys(d):
        plane = across(d)
        count = PLANE - 1 if d == 0 else PLANE
        wait_bytes(x_all.at[pl.ds(0, count * rows), :], x_recv_sem.at[plane])
        part = jnp.dot(x_all[plane_rows(plane), :], w_bf[...],
                       preferred_element_type=jnp.float32)
        part_f32[d] = part
        part_bf[d] = part.astype(jnp.bfloat16)
        for e, place in enumerate((last, core)):
            send(part_bf.at[d, block_rows(place), :], core_recv.at[d, e],
                 core_send_sem, core_recv_sem.at[d], at(z, core))

    def core_sum(d):
        wait_bytes(core_recv.at[d], core_recv_sem.at[d])
        pair_send[d] = (
            part_f32[d, block_rows(pair), :] + core_recv[d, 0].astype(jnp.float32)
        ).astype(jnp.bfloat16)
        send(pair_send.at[d], pair_recv.at[d], pair_send_sem, pair_recv_sem.at[d],
             at(z, pair))

    def plane_sum(d):
        summed = part_f32[d, block_rows(q), :] + core_recv[d, 1].astype(jnp.float32)
        wait_bytes(pair_recv.at[d], pair_recv_sem.at[d])
        summed += pair_recv[d].astype(jnp.float32)
        if d == 0:
            keys_acc[...] = summed
        else:
            keys_send[d - 1] = summed.astype(jnp.bfloat16)
            send(keys_send.at[d - 1], keys_recv.at[d - 1], keys_send_sem,
                 keys_recv_sem, at(across(d), q))

    turns = [0, *order]
    for step in range(planes + 2):
        if step < planes:
            partial_keys(turns[step])
        if 1 <= step <= planes:
            core_sum(turns[step - 1])
        if step >= 2:
            plane_sum(turns[step - 2])

    wait_bytes(delta_recv, delta_recv_sem)
    outer = delta_buf[...]
    for i in range(n_rep - 1):
        outer += delta_recv[i]
    outer_out[...] = outer

    wait_bytes(keys_recv, keys_recv_sem)
    keys = keys_acc[...]
    for d in range(planes - 1):
        keys += keys_recv[d].astype(jnp.float32)
    dproj_all[block_rows(me), :] = head_backward(
        keys * factor, cot_ref[...].astype(jnp.float32)
    )


    def pass_on(index, target):
        block = dproj_all.at[block_rows(index), :]
        send(block, block, dproj_send_sem, dproj_recv_sem.at[index], target)

    def arrived(index):
        wait_bytes(dproj_all.at[block_rows(index), :], dproj_recv_sem.at[index])

    for d in range(1, planes):
        pass_on(me, at(across(d), q))
    pass_on(me, at(z, pair))
    pass_on(me, at(z, core))

    def from_plane(d):
        index = at(across(d), q)
        arrived(index)
        pass_on(index, at(z, pair))
        pass_on(index, at(z, core))

    def from_pair(d):
        index = at(across(d), pair)
        arrived(index)
        pass_on(index, at(z, core))

    def add_plane(d):
        plane = across(d)
        arrived(at(plane, core))
        arrived(at(plane, last))
        product = lax.dot_general(
            x_all[plane_rows(plane), :], dproj_all[plane_rows(plane), :],
            (((0,), (0,)), ((), ())), preferred_element_type=jnp.float32,
        )
        if d == 0:
            grad_acc[...] = product
        else:
            grad_acc[...] += product

    for d in range(1, planes + 2):
        if d < planes:
            from_plane(d)
        if d - 1 < planes:
            from_pair(d - 1)
        if d >= 2:
            add_plane(d - 2)

    grad = grad_acc[...] * factor
    ones = jnp.ones((8, grad.shape[1]), jnp.float32)
    row = lax.dot_general(
        ones, w_bf[...].astype(jnp.float32) * grad, (((1,), (1,)), ((), ())),
        precision=lax.Precision.HIGHEST, preferred_element_type=jnp.float32,
    )[0:1, :]
    gain_own = gain_ref[:, pl.ds(pl.multiple_of(me * feats, feats), feats)]
    gain_buf[me] = gain_own - LR_GAIN * (row / gain_own)
    for i in range(1, n):
        send(gain_buf.at[me], gain_buf.at[me], gain_send_sem, gain_recv_sem,
             lax.rem(me + i, n))
    grad_out[...] = grad

    wait_bytes(normed_buf.at[pl.ds(0, n - 1)], x_send_sem)
    wait_bytes(core_recv, core_send_sem)
    wait_bytes(pair_recv, pair_send_sem)
    wait_bytes(keys_send, keys_send_sem)
    wait_bytes(dproj_all.at[pl.ds(0, (n - 1) * rows), :], dproj_send_sem)
    wait_bytes(delta_recv, delta_send_sem)
    wait_bytes(gain_buf.at[pl.ds(0, n - 1)], gain_recv_sem)
    for j in range(n):
        gain_out[:, j * feats:(j + 1) * feats] = gain_buf[j]
    wait_bytes(gain_buf.at[pl.ds(0, n - 1)], gain_send_sem)


def body(tokens, cotangent, gain, local_weight, stale_weight, global_weight, momentum):
    n = lax.axis_size("fsdp")
    n_rep = lax.axis_size("replica")
    rows, width = tokens.shape
    feats, units = global_weight.shape
    planes = n // PLANE
    factor = width ** (-0.5)
    f32, bf16 = jnp.float32, jnp.bfloat16
    vmem = pl.BlockSpec(memory_space=pltpu.VMEM)
    dma = pltpu.SemaphoreType.DMA
    weight = local_weight[0]
    weight_grad, gain_new, outer = pl.pallas_call(
        functools.partial(kernel, n, n_rep, factor),
        out_shape=(
            jax.ShapeDtypeStruct((feats, units), f32),
            jax.ShapeDtypeStruct((1, width), f32),
            jax.ShapeDtypeStruct((feats, units), f32),
        ),
        in_specs=[vmem] * 3 + [pl.BlockSpec(memory_space=pl.ANY)] * 3,
        out_specs=(vmem,) * 3,
        scratch_shapes=[
            pltpu.VMEM((feats, units), f32),
            pltpu.VMEM((feats, units), f32),
            pltpu.VMEM((feats, units), f32),
            pltpu.VMEM((n, rows, feats), bf16),
            pltpu.VMEM((n * rows, feats), bf16),
            pltpu.VMEM((feats, units), bf16),
            pltpu.VMEM((planes, PLANE * rows, units), f32),
            pltpu.VMEM((planes, PLANE * rows, units), bf16),
            pltpu.VMEM((planes, 2, rows, units), bf16),
            pltpu.VMEM((planes, rows, units), bf16),
            pltpu.VMEM((planes, rows, units), bf16),
            pltpu.VMEM((planes - 1, rows, units), bf16),
            pltpu.VMEM((planes - 1, rows, units), bf16),
            pltpu.VMEM((rows, units), f32),
            pltpu.VMEM((n * rows, units), bf16),
            pltpu.VMEM((feats, units), f32),
            pltpu.VMEM((feats, units), f32),
            pltpu.VMEM((n_rep - 1, feats, units), f32),
            pltpu.VMEM((n, 1, feats), f32),
            dma, dma((planes,)),
            dma, dma((planes,)),
            dma, dma((planes,)),
            dma, dma,
            dma, dma((n,)),
            dma, dma,
            dma, dma,
            dma((3,)),
        ],
        compiler_params=pltpu.CompilerParams(
            collective_id=0, has_side_effects=True, vmem_limit_bytes=58 * 1024 * 1024
        ),
        name="diloco_step",
    )(tokens, cotangent, gain, weight, stale_weight[0], global_weight)
    outer_mean = outer / n_rep
    momentum_new = MOMENT * momentum + outer_mean
    global_new = global_weight - LR_OUTER * (outer_mean + MOMENT * momentum_new)
    inner = weight - LR_INNER * weight_grad
    local_new = MIXING * inner + (1.0 - MIXING) * global_new
    return (local_new[None], gain_new, global_new, momentum_new)


def solution(mesh):
    return jax.shard_map(
        body,
        mesh=mesh,
        in_specs=(
            P(("replica", "fsdp"), None),
            P(("replica", "fsdp"), None),
            P("replica", None),
            P("replica", "fsdp", None),
            P("replica", "fsdp", None),
            P("fsdp", None),
            P("fsdp", None),
        ),
        out_specs=(
            P("replica", "fsdp", None),
            P("replica", None),
            P("fsdp", None),
            P("fsdp", None),
        ),
        check_vma=False,
    )
```

```python
import functools

import jax
import jax.numpy as jnp
from jax import lax
from jax.experimental import pallas as pl
from jax.experimental.pallas import tpu as pltpu
from jax.sharding import PartitionSpec as P

HEAD = 128
KV_HEADS = 4


EPS = 1e-05
LR_INNER = 0.3
LR_GAIN = 0.01
LR_OUTER = 0.7
MOMENT = 0.9
MIXING = 0.5

MESH = pl.DeviceIdType.MESH
PLANE = 4
HALVES = 2


def head_backward(keys, cot32):
    parts = []
    for h in range(KV_HEADS):
        cols = slice(h * HEAD, (h + 1) * HEAD)
        keys_h = keys[:, cols]
        cot_h = cot32[:, cols]
        key_scale = lax.rsqrt(jnp.mean(keys_h * keys_h, axis=1, keepdims=True) + EPS)
        unit_keys = keys_h * key_scale
        along = jnp.mean(cot_h * unit_keys, axis=1, keepdims=True)
        parts.append((key_scale * (cot_h - unit_keys * along)).astype(jnp.bfloat16))
    return jnp.concatenate(parts, axis=1)


def kernel(
    n, n_rep, factor,
    tok_ref, cot_ref, gain_ref, weight_hbm, stale_hbm, global_hbm,
    grad_out, gain_out, outer_out,
    weight_ref, stale_ref, global_ref,
    normed_buf, x_all, w_bf, part_f32, part_bf, core_recv, pair_send, pair_recv, keys_send, keys_recv,
    keys_acc, dproj_all, grad_acc, delta_buf, delta_recv, gain_buf,
    x_send_sem, x_recv_sem, core_send_sem, core_recv_sem, pair_send_sem, pair_recv_sem, keys_send_sem,
    keys_recv_sem, dproj_send_sem, dproj_recv_sem, delta_send_sem, delta_recv_sem,
    gain_send_sem, gain_recv_sem, load_sem,
):
    rep = lax.axis_index("replica")
    me = lax.axis_index("fsdp")
    planes = n // PLANE
    z, q = me // PLANE, me % PLANE
    pair = lax.rem(q + 2, PLANE)
    core = q + 1 - 2 * lax.rem(q, 2)
    last = lax.rem(core + 2, PLANE)
    rows = tok_ref.shape[0] // HALVES
    feats = weight_hbm.shape[0]

    def at(plane, place):
        return plane * PLANE + place

    def across(m):
        plane, bit = z, 1
        while bit < planes:
            if m & bit:
                plane = plane + bit - 2 * bit * lax.rem(z // bit, 2)
            bit *= 2
        return plane

    half = planes // 2
    order = [*range(half, planes), *range(1, half)]

    def send(src, dst, send_sem, recv_sem, target, replica=None):
        pltpu.make_async_remote_copy(
            src_ref=src, dst_ref=dst, send_sem=send_sem, recv_sem=recv_sem,
            device_id=(rep if replica is None else replica, target), device_id_type=MESH,
        ).start()

    def wait_bytes(ref, sem):
        pltpu.make_async_copy(ref, ref, sem).wait()

    barrier = pltpu.get_barrier_semaphore()
    for i in range(1, n):
        pl.semaphore_signal(
            barrier, inc=1, device_id=(rep, lax.rem(me + i, n)), device_id_type=MESH
        )
    for i in range(1, n_rep):
        pl.semaphore_signal(
            barrier, inc=1, device_id=(lax.rem(rep + i, n_rep), me), device_id_type=MESH
        )

    loads = [
        pltpu.make_async_copy(src, dst, load_sem.at[i])
        for i, (src, dst) in enumerate(
            ((weight_hbm, weight_ref), (stale_hbm, stale_ref), (global_hbm, global_ref))
        )
    ]
    for load in loads:
        load.start()

    total = jnp.zeros((rows * HALVES, 1), jnp.float32)
    for j in range(n):
        piece = tok_ref[:, j * feats:(j + 1) * feats].astype(jnp.float32)
        total += jnp.sum(piece * piece, axis=1, keepdims=True)
    inv_rms = lax.rsqrt(total / tok_ref.shape[1] + EPS)

    def normalize(index, h):
        cols = pl.ds(pl.multiple_of(index * feats, feats), feats)
        here = slice(h * rows, (h + 1) * rows)
        scaled = tok_ref[here, cols].astype(jnp.float32) * inv_rms[here]
        return (scaled * gain_ref[:, cols]).astype(jnp.bfloat16)

    pl.semaphore_wait(barrier, n - 1 + n_rep - 1)

    def block_rows(index):
        return pl.ds(pl.multiple_of(index * rows, rows), rows)

    def plane_rows(plane):
        return pl.ds(pl.multiple_of(plane * (PLANE * rows), PLANE * rows), PLANE * rows)

    for h in range(HALVES):
        for d in [*order, 0]:
            for e in range(PLANE):
                if d == 0 and e == 0:
                    continue
                target = at(across(d), lax.rem(q + e, PLANE))
                normed_buf[h, target] = normalize(target, h)
                send(normed_buf.at[h, target], x_all.at[h, block_rows(me), :],
                     x_send_sem.at[h], x_recv_sem.at[h, z], target)
    for load in loads:
        load.wait()
    delta_buf[...] = global_ref[...] - stale_ref[...]
    for i in range(1, n_rep):
        send(delta_buf, delta_recv.at[i - 1], delta_send_sem, delta_recv_sem, me,
             lax.rem(rep + i, n_rep))
    for h in range(HALVES):
        x_all[h, block_rows(me), :] = normalize(me, h)
    w_bf[...] = weight_ref[...].astype(jnp.bfloat16)

    def partial_keys(h, d):
        plane = across(d)
        count = PLANE - 1 if d == 0 else PLANE
        wait_bytes(x_all.at[h, pl.ds(0, count * rows), :], x_recv_sem.at[h, plane])
        part = jnp.dot(x_all[h, plane_rows(plane), :], w_bf[...],
                       preferred_element_type=jnp.float32)
        part_f32[h, d] = part
        part_bf[h, d] = part.astype(jnp.bfloat16)
        for e, place in enumerate((last, core)):
            send(part_bf.at[h, d, block_rows(place), :], core_recv.at[h, d, e],
                 core_send_sem.at[h], core_recv_sem.at[h, d], at(z, core))

    def core_sum(h, d):
        wait_bytes(core_recv.at[h, d], core_recv_sem.at[h, d])
        pair_send[h, d] = (
            part_f32[h, d, block_rows(pair), :] + core_recv[h, d, 0].astype(jnp.float32)
        ).astype(jnp.bfloat16)
        send(pair_send.at[h, d], pair_recv.at[h, d], pair_send_sem.at[h], pair_recv_sem.at[h, d],
             at(z, pair))

    def plane_sum(h, d):
        summed = part_f32[h, d, block_rows(q), :] + core_recv[h, d, 1].astype(jnp.float32)
        wait_bytes(pair_recv.at[h, d], pair_recv_sem.at[h, d])
        summed += pair_recv[h, d].astype(jnp.float32)
        if d == 0:
            keys_acc[h] = summed
        else:
            keys_send[h, d - 1] = summed.astype(jnp.bfloat16)
            send(keys_send.at[h, d - 1], keys_recv.at[h, d - 1], keys_send_sem.at[h],
                 keys_recv_sem.at[h], at(across(d), q))


    def pass_on(h, index, target):
        block = dproj_all.at[h, block_rows(index), :]
        send(block, block, dproj_send_sem.at[h], dproj_recv_sem.at[h, index], target)

    def arrived(h, index):
        wait_bytes(dproj_all.at[h, block_rows(index), :], dproj_recv_sem.at[h, index])

    def from_plane(h, d):
        index = at(across(d), q)
        arrived(h, index)
        pass_on(h, index, at(z, pair))
        pass_on(h, index, at(z, core))

    def from_pair(h, d):
        index = at(across(d), pair)
        arrived(h, index)
        pass_on(h, index, at(z, core))

    def add_plane(h, d):
        plane = across(d)
        arrived(h, at(plane, core))
        arrived(h, at(plane, last))
        product = lax.dot_general(
            x_all[h, plane_rows(plane), :], dproj_all[h, plane_rows(plane), :],
            (((0,), (0,)), ((), ())), preferred_element_type=jnp.float32,
        )
        if h == 0 and d == 0:
            grad_acc[...] = product
        else:
            grad_acc[...] += product

    def sum_keys(h):
        turns = [0, *order]
        for step in range(planes + 2):
            if step < planes:
                partial_keys(h, turns[step])
            if 1 <= step <= planes:
                core_sum(h, turns[step - 1])
            if step >= 2:
                plane_sum(h, turns[step - 2])

    def start_gather(h):
        wait_bytes(keys_recv.at[h], keys_recv_sem.at[h])
        keys = keys_acc[h]
        for d in range(planes - 1):
            keys += keys_recv[h, d].astype(jnp.float32)
        dproj_all[h, block_rows(me), :] = head_backward(
            keys * factor, cot_ref[h * rows:(h + 1) * rows, :].astype(jnp.float32)
        )

        for d in order:
            pass_on(h, me, at(across(d), q))
        pass_on(h, me, at(z, pair))
        pass_on(h, me, at(z, core))

    def forward(h):
        from_pair(h, 0)
        for d in order:
            from_plane(h, d)
        for d in order:
            from_pair(h, d)

    def add_products(h):
        for d in (0, *order):
            add_plane(h, d)

    sum_keys(0)
    start_gather(0)
    for h in range(1, HALVES):
        sum_keys(h)
        forward(h - 1)
        start_gather(h)
        add_products(h - 1)
    wait_bytes(delta_recv, delta_recv_sem)
    outer = delta_buf[...]
    for i in range(n_rep - 1):
        outer += delta_recv[i]
    outer_out[...] = outer

    forward(HALVES - 1)
    add_products(HALVES - 1)

    grad = grad_acc[...] * factor
    ones = jnp.ones((8, grad.shape[1]), jnp.float32)
    row = lax.dot_general(
        ones, w_bf[...].astype(jnp.float32) * grad, (((1,), (1,)), ((), ())),
        precision=lax.Precision.HIGHEST, preferred_element_type=jnp.float32,
    )[0:1, :]
    gain_own = gain_ref[:, pl.ds(pl.multiple_of(me * feats, feats), feats)]
    gain_buf[me] = gain_own - LR_GAIN * (row / gain_own)
    for i in range(1, n):
        send(gain_buf.at[me], gain_buf.at[me], gain_send_sem, gain_recv_sem,
             lax.rem(me + i, n))
    grad_out[...] = grad

    for h in range(HALVES):
        wait_bytes(normed_buf.at[h, pl.ds(0, n - 1)], x_send_sem.at[h])
        wait_bytes(core_recv.at[h], core_send_sem.at[h])
        wait_bytes(pair_recv.at[h], pair_send_sem.at[h])
        wait_bytes(keys_send.at[h], keys_send_sem.at[h])
        wait_bytes(dproj_all.at[h, pl.ds(0, (n - 1) * rows), :], dproj_send_sem.at[h])
    wait_bytes(delta_recv, delta_send_sem)
    wait_bytes(gain_buf.at[pl.ds(0, n - 1)], gain_recv_sem)
    for j in range(n):
        gain_out[:, j * feats:(j + 1) * feats] = gain_buf[j]
    wait_bytes(gain_buf.at[pl.ds(0, n - 1)], gain_send_sem)


def body(tokens, cotangent, gain, local_weight, stale_weight, global_weight, momentum):
    n = lax.axis_size("fsdp")
    n_rep = lax.axis_size("replica")
    width = tokens.shape[1]
    rows = tokens.shape[0] // HALVES
    feats, units = global_weight.shape
    planes = n // PLANE
    factor = width ** (-0.5)
    f32, bf16 = jnp.float32, jnp.bfloat16
    vmem = pl.BlockSpec(memory_space=pltpu.VMEM)
    dma = pltpu.SemaphoreType.DMA
    weight = local_weight[0]
    weight_grad, gain_new, outer = pl.pallas_call(
        functools.partial(kernel, n, n_rep, factor),
        out_shape=(
            jax.ShapeDtypeStruct((feats, units), f32),
            jax.ShapeDtypeStruct((1, width), f32),
            jax.ShapeDtypeStruct((feats, units), f32),
        ),
        in_specs=[vmem] * 3 + [pl.BlockSpec(memory_space=pl.ANY)] * 3,
        out_specs=(vmem,) * 3,
        scratch_shapes=[
            pltpu.VMEM((feats, units), f32),
            pltpu.VMEM((feats, units), f32),
            pltpu.VMEM((feats, units), f32),
            pltpu.VMEM((HALVES, n, rows, feats), bf16),
            pltpu.VMEM((HALVES, n * rows, feats), bf16),
            pltpu.VMEM((feats, units), bf16),
            pltpu.VMEM((HALVES, planes, PLANE * rows, units), f32),
            pltpu.VMEM((HALVES, planes, PLANE * rows, units), bf16),
            pltpu.VMEM((HALVES, planes, 2, rows, units), bf16),
            pltpu.VMEM((HALVES, planes, rows, units), bf16),
            pltpu.VMEM((HALVES, planes, rows, units), bf16),
            pltpu.VMEM((HALVES, planes - 1, rows, units), bf16),
            pltpu.VMEM((HALVES, planes - 1, rows, units), bf16),
            pltpu.VMEM((HALVES, rows, units), f32),
            pltpu.VMEM((HALVES, n * rows, units), bf16),
            pltpu.VMEM((feats, units), f32),
            pltpu.VMEM((feats, units), f32),
            pltpu.VMEM((n_rep - 1, feats, units), f32),
            pltpu.VMEM((n, 1, feats), f32),
            dma((HALVES,)), dma((HALVES, planes)),
            dma((HALVES,)), dma((HALVES, planes)),
            dma((HALVES,)), dma((HALVES, planes)),
            dma((HALVES,)), dma((HALVES,)),
            dma((HALVES,)), dma((HALVES, n)),
            dma, dma,
            dma, dma,
            dma((3,)),
        ],
        compiler_params=pltpu.CompilerParams(
            collective_id=0, has_side_effects=True, vmem_limit_bytes=58 * 1024 * 1024
        ),
        name="diloco_step",
    )(tokens, cotangent, gain, weight, stale_weight[0], global_weight)
    outer_mean = outer / n_rep
    momentum_new = MOMENT * momentum + outer_mean
    global_new = global_weight - LR_OUTER * (outer_mean + MOMENT * momentum_new)
    inner = weight - LR_INNER * weight_grad
    local_new = MIXING * inner + (1.0 - MIXING) * global_new
    return (local_new[None], gain_new, global_new, momentum_new)


def solution(mesh):
    return jax.shard_map(
        body,
        mesh=mesh,
        in_specs=(
            P(("replica", "fsdp"), None),
            P(("replica", "fsdp"), None),
            P("replica", None),
            P("replica", "fsdp", None),
            P("replica", "fsdp", None),
            P("fsdp", None),
            P("fsdp", None),
        ),
        out_specs=(
            P("replica", "fsdp", None),
            P("replica", None),
            P("fsdp", None),
            P("fsdp", None),
        ),
        check_vma=False,
    )
```
